32 devices in a mesh: grp: 1, gx: 16 (over z, y, x), gy: 2 (over core).
Axes of the slice: x: 2, y: 2, z: 4, core: 2. Of those that a mesh axis runs over, the one named last changes fastest.
Arguments:
- field: bfloat16 [8, 256, 512, 256], P(None, ('grp', 'gx'), 'gy'), may hold values from -20 to 20, as said below
- factor_x_old: bfloat16 [256, 32], P(('grp', 'gx')), may hold values from -0.375 to 0.375
- factor_y_old: bfloat16 [512, 32], P(('grp', 'gy')), may hold values from -0.25 to 0.25
- factor_z: bfloat16 [256, 32], replicated, may hold values from -0.375 to 0.375
- factor_t: bfloat16 [8, 4], replicated, may hold values from -2 to 2
Outputs:
- factor_x: float32 [256, 32], P(('grp', 'gx'))
- factor_y: float32 [512, 32], P(('grp', 'gy'))
- core: float32 [4096, 32], P(('grp', 'gx', 'gy'))
The draws below stay inside these ranges and needn't reach their ends.
Inputs may be any that keep to these rules, and one draw needn't show every extreme that they name: A field of order one whose magnitude varies across the grid.
All inputs are finite; a program needn't handle non-finite values.
Results may differ from the reference program's by a relative error of at most 0.002.
Values may be sent and summed in bfloat16 or wider, within the bound.
A program may use at most 64 MiB of HBM per device.

```python
import math
import jax
import jax.numpy as jnp
from jax import lax

NX = 256
NZ = 256
NT = 8
RX = 32
RY = 32
RZ = 32
RT = 4
NY = 512


def draw_field(key, part):
    key = jax.random.fold_in(key, 11)
    first = jax.random.fold_in(key, 0)
    place = jnp.arange(NX, dtype=jnp.float32) / NX
    rising = (3.0 ** place)[None, :, None, None]
    values = jax.random.truncated_normal(first, -6.0, 6.0, (NT, NX, NY, NZ), jnp.float32) * rising
    return values.astype(jnp.bfloat16)


def levels(stream_key, extent, shards, smallest, largest):
    def one(axis_at, shards_of):
        steps = jax.random.uniform(jax.random.fold_in(jax.random.fold_in(stream_key, 6), axis_at), (shards_of,), jnp.float32, smallest / len(shards), largest / len(shards))
        return jnp.repeat(jnp.exp(steps), extent[axis_at] // shards_of).reshape((-1,) + (1,) * (len(extent) - axis_at - 1))

    level = one(*shards[0])
    for cut in shards[1:]:
        level = level * one(*cut)
    return level


def gaussian(own_key, dims, scale, reach, shards=(), kind=jnp.bfloat16):
    result = jax.random.normal(own_key, dims, jnp.float32) * scale
    if len(shards) > 0:
        result = levels(own_key, dims, shards, -0.22, 0.18) * result
    return jnp.clip(result, min=-reach, max=reach).astype(kind)


def setup_inputs(seed: int = 0, part: int = 0) -> dict:
    seeds = jax.random.split(jax.random.key(seed), 6)
    own_keys = jax.random.split(jax.random.fold_in(seeds[5], part), 6)
    field = draw_field(jax.random.fold_in(jax.random.fold_in(seeds[5], part), 71), part)
    factor_x_old = gaussian(own_keys[1], (NX, RX), NX ** -0.5, 0.375, ((0, 16),))
    factor_y_old = gaussian(own_keys[2], (NY, RY), NY ** -0.5, 0.25, ((0, 2),))
    factor_z = gaussian(seeds[3], (NZ, RZ), NZ ** -0.5, 0.375)
    factor_t = gaussian(seeds[4], (NT, RT), NT ** -0.5, 2.0)
    return {"field": field, "factor_x_old": factor_x_old, "factor_y_old": factor_y_old, "factor_z": factor_z, "factor_t": factor_t}


def orthonormal(power):
    highest = lax.Precision.HIGHEST
    gram = jnp.dot(power.T, power, precision=highest)
    lower = jnp.linalg.cholesky(gram)
    return jax.scipy.linalg.solve_triangular(lower, power.T, lower=True).T

def reference(field, factor_x_old, factor_y_old, factor_z, factor_t):
    highest = lax.Precision.HIGHEST
    partial_q = jnp.einsum('txyz,zc->txcy', field.astype(jnp.float32), factor_z.astype(jnp.float32), preferred_element_type=jnp.float32)
    projected = jnp.einsum('td,txcy->dxcy', factor_t.astype(jnp.float32), partial_q, precision=highest)
    mode_rows = jnp.einsum('dxcy,yb->xdcb', projected, factor_y_old.astype(jnp.float32), precision=highest)
    mode_rows = mode_rows.reshape(NX, RT * RZ * RY).astype(jnp.bfloat16)
    mode_float = mode_rows.astype(jnp.float32)
    inner = jnp.dot(mode_float.T, factor_x_old.astype(jnp.float32), precision=highest)
    power_x = jnp.dot(mode_float, inner, precision=highest)
    basis_x = orthonormal(power_x)
    core_x = jnp.dot(basis_x.T, mode_float, precision=highest)
    spread = jnp.dot(basis_x, core_x, precision=highest).reshape(NX, RT, RZ, RY)
    power_y = jnp.einsum('dxcy,xdcb->yb', projected, spread, precision=highest)
    basis_y = orthonormal(power_y)
    folded = jnp.einsum('dxcy,yb->dxcb', projected, basis_y, precision=highest)
    core = jnp.einsum('dxcb,xa->dcab', folded, basis_x, precision=highest).reshape(RT * RZ * RX, RY)
    return (math.sqrt(NX) * basis_x, math.sqrt(NY) * basis_y, core)
```

```python
import functools
import math

import jax
import jax.numpy as jnp
from jax import lax
from jax.experimental import pallas as pl
from jax.experimental.pallas import tpu as pltpu
from jax.sharding import PartitionSpec as P

MESH = pl.DeviceIdType.MESH
HIGH = lax.Precision.HIGHEST
F32 = jnp.float32
BF16 = jnp.bfloat16
LANES = 128
NN = (((1,), (0,)), ((), ()))
NT = (((1,), (1,)), ((), ()))
TN = (((0,), (0,)), ((), ()))


def mm(a, b, dims, precision=None):
    return lax.dot_general(a, b, dims, precision=precision, preferred_element_type=F32)


def split2(v):
    hi = v.astype(BF16)
    return hi, (v - hi.astype(F32)).astype(BF16)


def split3(v):
    hi = v.astype(BF16)
    rest = v - hi.astype(F32)
    mid = rest.astype(BF16)
    return hi, mid, (rest - mid.astype(F32)).astype(BF16)


def inverse_lower(gram):
    n = gram.shape[0]
    row = lax.broadcasted_iota(jnp.int32, (n, n), 0)
    col = lax.broadcasted_iota(jnp.int32, (n, n), 1)
    eye = jnp.where(row == col, 1.0, 0.0).astype(F32)
    both = jnp.concatenate([gram, eye], axis=1)
    at = lax.broadcasted_iota(jnp.int32, (n, 1), 0)
    for j in range(n - 1):
        pivot_row = both[j : j + 1, :]
        scale = jnp.where(at > j, both[:, j : j + 1] / pivot_row[:, j : j + 1], 0.0)
        both = both - scale * pivot_row
    diag = jnp.sum(both[:, :n] * eye, axis=1, keepdims=True)
    return both[:, n:] * lax.rsqrt(diag)


def project_kernel(field_ref, fz_ref, ft_ref, fy_ref, pp_ref, a_ref, w_ref, fyt_ref):
    steps = field_ref.shape[0]

    @pl.when(pl.program_id(0) == 0)
    def _():
        for t in range(steps):
            hi, lo = split2(fz_ref[...] * ft_ref[t : t + 1, :])
            w_ref[t, :, :LANES] = hi
            w_ref[t, :, LANES:] = lo
        fyt_ref[...] = fy_ref[...].astype(F32).T.astype(BF16)

    acc = mm(field_ref[0, 0], w_ref[0], NN)
    for t in range(1, steps):
        acc = acc + mm(field_ref[t, 0], w_ref[t], NN)
    hi, lo = split2(acc[:, :LANES] + acc[:, LANES:])
    pp = jnp.concatenate([hi, lo], axis=1)
    pp_ref[0] = pp
    rows = mm(fyt_ref[...], pp, NN)
    a_ref[0] = rows[:, :LANES] + rows[:, LANES:]


def tucker_kernel(
    chips, scale_x, scale_y,
    pp_ref, a_ref, fx_ref,
    fx_out, fy_out, core_out,
    part, other, y_all, qx_ref, s3, wy_send, wy_recv, my_send, my_recv, fold, fold2, shares, pair_in, mine, landed,
    pair_sem, gather_send, gather_recv, give_send, give_recv, wy_sem, core_send, core_recv,
):
    grp = lax.axis_index("grp")
    g = lax.axis_index("gx")
    h = lax.axis_index("gy")
    z = g // 4
    p = g % 4
    nx = a_ref.shape[0]
    nb = a_ref.shape[1]
    half = nb // 2 * LANES
    xs = chips * nx
    partner = (grp, g, 1 - h)

    def peer(chip):
        return (grp, chip, h)

    barrier = pltpu.get_barrier_semaphore()
    pl.semaphore_signal(barrier, inc=1, device_id=partner, device_id_type=MESH)
    for k in range(1, chips):
        pl.semaphore_signal(barrier, inc=1, device_id=peer((g + k) % chips), device_id_type=MESH)
    for b in range(nb):
        part[:, b * LANES : (b + 1) * LANES] = a_ref[:, b, :]
    pl.semaphore_wait(barrier, chips)

    swap = pltpu.make_async_remote_copy(
        part, other, pair_sem.at[0], pair_sem.at[1], device_id=partner, device_id_type=MESH
    )
    swap.start()
    own = pl.ds(pl.multiple_of(g * nx, nx), nx)
    for s in range(2):
        y_all[s, own, half:] = jnp.zeros((nx, LANES), BF16)
        y_all[s, own, half : half + fx_ref.shape[1]] = fx_ref[...]
    swap.wait()
    for s in range(2):
        at = slice(s * half, (s + 1) * half)
        y_all[s, own, :half] = (part[:, at] + other[:, at]).astype(BF16)

    def block(chip, side):
        return y_all.at[side, pl.ds(pl.multiple_of(chip * nx, nx), nx), :]

    def chip_of(q, k):
        return ((z + 4 - k) % 4) * 4 + (p + q) % 4

    def gather(q, k, target, source):
        i = q * 4 + k
        return pltpu.make_async_remote_copy(
            block(source, h), block(source, h), gather_send.at[i], gather_recv.at[i],
            device_id=peer(target), device_id_type=MESH,
        )

    def give(q, k):
        i = q * 4 + k
        source = chip_of(q, k)
        return pltpu.make_async_remote_copy(
            block(source, h), block(source, h), give_send.at[i], give_recv.at[i],
            device_id=partner, device_id_type=MESH,
        )

    started = []
    for k in (1, 3, 2):
        c = gather(0, k, ((z + k) % 4) * 4 + p, g)
        c.start()
        started.append(c)
    for q in (1, 3, 2):
        c = gather(q, 0, z * 4 + (p + 4 - q) % 4, g)
        c.start()
        started.append(c)
    gives = []

    def arrived(q, k):
        i = q * 4 + k
        source = chip_of(q, k)
        pltpu.make_async_remote_copy(
            block(source, h), block(source, h), gather_send.at[i], gather_recv.at[i],
            device_id=partner, device_id_type=MESH,
        ).wait_recv()
        c = give(q, k)
        c.start()
        gives.append((c, q, k))

    for k in (1, 3, 2):
        arrived(0, k)
        for q in (1, 3, 2):
            c = gather(q, k, z * 4 + (p + 4 - q) % 4, chip_of(0, k))
            c.start()
            started.append(c)
    for k in (0, 1, 3, 2):
        for q in (1, 3, 2):
            arrived(q, k)
    for c, q, k in gives:
        i = q * 4 + k
        theirs = block(chip_of(q, k), 1 - h)
        pltpu.make_async_remote_copy(
            theirs, theirs, give_send.at[i], give_recv.at[i], device_id=partner, device_id_type=MESH
        ).wait_recv()
    for c in started:
        c.wait_send()
    for c, q, k in gives:
        c.wait_send()

    left = y_all[0, :, :half]
    right = y_all[1, :, :half]
    gram = mm(left, left, NT) + mm(right, right, NT)
    old = y_all[0, :, half:][:, : fx_ref.shape[1]].astype(F32)
    power_x = mm(gram, old, NN, HIGH)
    inv_x = inverse_lower(mm(power_x, power_x, TN, HIGH))
    qx = mm(power_x, inv_x, NT, HIGH)
    qx_ref[...] = qx
    q_own = qx_ref[own, :]
    fx_out[...] = scale_x * q_own
    onto = jnp.concatenate(split3(mm(q_own, qx, NT, HIGH)), axis=0)
    for s in range(2):
        spread = mm(onto, y_all[s, :, :half], NN)
        spread = spread[:nx] + spread[nx : 2 * nx] + spread[2 * nx :]
        for b in range(nb // 2):
            s3[s * (nb // 2) + b] = spread[:, b * LANES : (b + 1) * LANES]

    acc = jnp.zeros((2 * nb, pp_ref.shape[1]), F32)
    for x in range(nx):
        hi, lo = split2(s3[:, x, :])
        both = jnp.concatenate([jnp.concatenate([hi, hi], 1), jnp.concatenate([lo, lo], 1)], 0)
        acc = acc + mm(both, pp_ref[x], NT)
    power_y = acc[:nb] + acc[nb:]
    for i, flip in enumerate((1, 2, 4, 8)):
        low = g % (2 * flip)
        target = jnp.where(low < flip, g + flip, g - flip)
        wy_send[i] = power_y
        c = pltpu.make_async_remote_copy(
            wy_send.at[i], wy_recv.at[i], wy_sem.at[0, i], wy_sem.at[1, i],
            device_id=peer(target), device_id_type=MESH,
        )
        c.start()
        c.wait()
        power_y = power_y + wy_recv[i]

    my_send[...] = jnp.zeros(my_send.shape, F32)
    my_send[:, :nb] = mm(power_y, power_y, NT, HIGH)
    my_copy = pltpu.make_async_remote_copy(
        my_send, my_recv, pair_sem.at[2], pair_sem.at[3], device_id=partner, device_id_type=MESH
    )
    my_copy.start()

    wy2 = jnp.concatenate(split2(power_y), axis=0)
    for x in range(nx):
        f = mm(wy2, pp_ref[x], NN)
        f = f[:nb] + f[nb:]
        fold[x] = f[:, :LANES] + f[:, LANES:]
    for b in range(nb):
        fold2[:, b * LANES : (b + 1) * LANES] = fold[:, b, :]
    term = mm(q_own, fold2[...], TN, HIGH)
    for r in range(8):
        rows = jnp.concatenate(
            [term[:, (u * 8 + r) * LANES : (u * 8 + r + 1) * LANES] for u in range(nb // 8)], axis=0
        )
        shares[:, r, :] = rows.T
    mine_rows = shares.shape[0] // (2 * chips)
    pair_copies = []
    for c in range(chips):
        src = shares.at[pl.ds((c * 2 + 1 - h) * mine_rows, mine_rows)]
        cp = pltpu.make_async_remote_copy(
            src, pair_in.at[c], core_send.at[0, c], core_recv.at[0, c],
            device_id=partner, device_id_type=MESH,
        )
        cp.start()
        pair_copies.append(cp)
    for cp in pair_copies:
        cp.wait()
    for c in range(chips):
        mine[c] = shares[pl.ds((c * 2 + h) * mine_rows, mine_rows)] + pair_in[c]
    sends = []
    for k in range(1, chips):
        target = (g + k) % chips
        cp = pltpu.make_async_remote_copy(
            mine.at[target], landed.at[k], core_send.at[1, k], core_recv.at[1, k],
            device_id=peer(target), device_id_type=MESH,
        )
        cp.start()
        sends.append(cp)

    my_copy.wait()
    inv_y = inverse_lower(my_send[:, :nb] + my_recv[:, :nb])
    fy_out[...] = scale_y * mm(power_y, inv_y, (((0,), (1,)), ((), ())), HIGH)

    for cp in sends:
        cp.wait()
    total = mine[g]
    for k in range(1, chips):
        total = total + landed[k]
    ra = fx_ref.shape[1]
    columns = [
        jnp.concatenate([total[i][:, u * ra : (u + 1) * ra] for u in range(nb // 8)], axis=0)
        for i in range(mine_rows)
    ]
    raw = jnp.concatenate(columns, axis=1)
    core_out[...] = mm(raw, inv_y, (((0,), (1,)), ((), ())), HIGH)


def fast_body(chips, field, factor_x_old, factor_y_old, factor_z, factor_t):
    nt, nx, ny, nz = field.shape
    ra = factor_x_old.shape[1]
    nb = factor_y_old.shape[1]
    nc = factor_z.shape[1]
    nd = factor_t.shape[1]
    fz = jnp.tile(factor_z.astype(F32), (1, nd))
    ft = jnp.repeat(factor_t.astype(F32), nc, axis=1)
    whole = lambda shape: pl.BlockSpec(shape, lambda x: (0,) * len(shape))
    pp, a = pl.pallas_call(
        project_kernel,
        grid=(nx,),
        in_specs=[
            pl.BlockSpec((nt, 1, ny, nz), lambda x: (0, x, 0, 0)),
            whole((nz, LANES)), whole((nt, LANES)), whole((ny, nb)),
        ],
        out_specs=[
            pl.BlockSpec((1, ny, 2 * LANES), lambda x: (x, 0, 0)),
            pl.BlockSpec((1, nb, LANES), lambda x: (x, 0, 0)),
        ],
        out_shape=[
            jax.ShapeDtypeStruct((nx, ny, 2 * LANES), BF16),
            jax.ShapeDtypeStruct((nx, nb, LANES), F32),
        ],
        scratch_shapes=[pltpu.VMEM((nt, nz, 2 * LANES), BF16), pltpu.VMEM((nb, ny), BF16)],
        compiler_params=pltpu.CompilerParams(
            dimension_semantics=("arbitrary",), vmem_limit_bytes=32 << 20
        ),
    )(field, fz, ft, factor_y_old)
    xs = nx * chips
    wide = nb * LANES
    rows = LANES // (2 * chips)
    vmem = pl.BlockSpec(memory_space=pltpu.VMEM)
    dma = pltpu.SemaphoreType.DMA
    return pl.pallas_call(
        functools.partial(tucker_kernel, chips, math.sqrt(xs), math.sqrt(2 * ny)),
        in_specs=[vmem] * 3,
        out_specs=[vmem] * 3,
        out_shape=[
            jax.ShapeDtypeStruct((nx, ra), F32),
            jax.ShapeDtypeStruct((ny, nb), F32),
            jax.ShapeDtypeStruct((rows * ra, nb), F32),
        ],
        scratch_shapes=[
            pltpu.VMEM((nx, wide), F32),
            pltpu.VMEM((nx, wide), F32),
            pltpu.VMEM((2, xs, wide // 2 + LANES), BF16),
            pltpu.VMEM((xs, ra), F32),
            pltpu.VMEM((nb, nx, LANES), F32),
            pltpu.VMEM((4, nb, ny), F32),
            pltpu.VMEM((4, nb, ny), F32),
            pltpu.VMEM((nb, LANES), F32),
            pltpu.VMEM((nb, LANES), F32),
            pltpu.VMEM((nx, nb, LANES), F32),
            pltpu.VMEM((nx, wide), F32),
            pltpu.VMEM((LANES, 8, LANES), F32),
            pltpu.VMEM((chips, rows, 8, LANES), F32),
            pltpu.VMEM((chips, rows, 8, LANES), F32),
            pltpu.VMEM((chips, rows, 8, LANES), F32),
            dma((4,)), dma((16,)), dma((16,)), dma((16,)), dma((16,)), dma((2, 4)), dma((2, chips)), dma((2, chips)),
        ],
        compiler_params=pltpu.CompilerParams(
            collective_id=0, has_side_effects=True, vmem_limit_bytes=40 << 20
        ),
    )(pp, a, factor_x_old)


def orthonormal(power, gram):
    lower = jnp.linalg.cholesky(gram)
    return jax.scipy.linalg.solve_triangular(lower, power.T, lower=True).T


def body(field, factor_x_old, factor_y_old, factor_z, factor_t):
    highest = lax.Precision.HIGHEST
    rows_x = field.shape[1]
    rank_x = factor_x_old.shape[1]
    rank_y = factor_y_old.shape[1]
    rank_z = factor_z.shape[1]
    rank_t = factor_t.shape[1]
    partial_q = jnp.einsum("txyz,zc->txcy", field, factor_z, preferred_element_type=jnp.float32)
    projected = jnp.einsum(
        "td,txcy->dxcy", factor_t.astype(jnp.float32), partial_q, precision=highest
    )
    local_rows = jnp.einsum(
        "dxcy,yb->xdcb", projected, factor_y_old.astype(jnp.float32), precision=highest
    )
    local_rows = local_rows.reshape(rows_x, rank_t * rank_z * rank_y)
    summed = lax.psum(local_rows, "gy")
    mode_rows = summed.astype(jnp.bfloat16)
    mode_float = mode_rows.astype(jnp.float32)
    gram = lax.dot_general(
        mode_rows,
        lax.all_gather(mode_rows, "gx", axis=0, tiled=True),
        (((1,), (1,)), ((), ())),
        preferred_element_type=jnp.float32,
    )
    power_x = jnp.dot(
        gram,
        lax.all_gather(factor_x_old, "gx", axis=0, tiled=True).astype(jnp.float32),
        precision=highest,
    )
    gram_x = lax.psum(jnp.dot(power_x.T, power_x, precision=highest), "gx")
    basis_x = orthonormal(power_x, gram_x)
    core_x = lax.psum(jnp.dot(basis_x.T, mode_float, precision=highest), "gx")
    spread = jnp.dot(basis_x, core_x, precision=highest).reshape(rows_x, rank_t, rank_z, rank_y)
    part_y = jnp.einsum("dxcy,xdcb->yb", projected, spread, precision=highest)
    power_y = lax.psum(part_y, "gx")
    gram_y = lax.psum(jnp.dot(power_y.T, power_y, precision=highest), "gy")
    basis_y = orthonormal(power_y, gram_y)
    folded = jnp.einsum("dxcy,yb->dxcb", projected, basis_y, precision=highest)
    core_term = jnp.einsum("dxcb,xa->dcab", folded, basis_x, precision=highest).reshape(
        rank_t * rank_z * rank_x, rank_y
    )
    core = lax.psum_scatter(core_term, ("gx", "gy"), scatter_dimension=0, tiled=True)
    total_x = rows_x * lax.axis_size("gx")
    total_y = power_y.shape[0] * lax.axis_size("gy")
    return (math.sqrt(total_x) * basis_x, math.sqrt(total_y) * basis_y, core)


def solution(mesh):
    placed = (
        P(None, ("grp", "gx"), "gy", None),
        P(("grp", "gx"), None),
        P(("grp", "gy"), None),
        P(),
        P(),
    )
    chips = mesh.shape["gx"]

    def run(field, factor_x_old, factor_y_old, factor_z, factor_t):
        packed = factor_z.shape[1] * factor_t.shape[1]
        fits = (
            chips == 16
            and mesh.shape["gy"] == 2
            and packed == LANES
            and field.shape[1] == 16
            and factor_x_old.shape[1] == 32
            and factor_y_old.shape[1] == 32
            and field.shape[2] % 256 == 0
            and field.shape[3] % 256 == 0
        )
        if fits:
            return fast_body(chips, field, factor_x_old, factor_y_old, factor_z, factor_t)
        return body(field, factor_x_old, factor_y_old, factor_z, factor_t)

    return jax.shard_map(
        run,
        mesh=mesh,
        in_specs=placed,
        out_specs=(P(("grp", "gx"), None), P(("grp", "gy"), None), P(("grp", "gx", "gy"), None)),
        check_vma=False,
    )
```

```python
import functools
import math

import jax
import jax.numpy as jnp
from jax import lax
from jax.experimental import pallas as pl
from jax.experimental.pallas import tpu as pltpu
from jax.sharding import PartitionSpec as P

MESH = pl.DeviceIdType.MESH
HIGH = lax.Precision.HIGHEST
F32 = jnp.float32
BF16 = jnp.bfloat16
LANES = 128
NN = (((1,), (0,)), ((), ()))
NT = (((1,), (1,)), ((), ()))
TN = (((0,), (0,)), ((), ()))


def mm(a, b, dims, precision=None):
    return lax.dot_general(a, b, dims, precision=precision, preferred_element_type=F32)


def split2(v):
    hi = v.astype(BF16)
    return hi, (v - hi.astype(F32)).astype(BF16)


def split3(v):
    hi = v.astype(BF16)
    rest = v - hi.astype(F32)
    mid = rest.astype(BF16)
    return hi, mid, (rest - mid.astype(F32)).astype(BF16)


def inverse_lower(gram):
    n = gram.shape[0]
    row = lax.broadcasted_iota(jnp.int32, (n, n), 0)
    col = lax.broadcasted_iota(jnp.int32, (n, n), 1)
    eye = jnp.where(row == col, 1.0, 0.0).astype(F32)
    both = jnp.concatenate([gram, eye], axis=1)
    at = lax.broadcasted_iota(jnp.int32, (n, 1), 0)
    for j in range(n - 1):
        pivot_row = both[j : j + 1, :]
        scale = jnp.where(at > j, both[:, j : j + 1] / pivot_row[:, j : j + 1], 0.0)
        both = both - scale * pivot_row
    diag = jnp.sum(both[:, :n] * eye, axis=1, keepdims=True)
    return both[:, n:] * lax.rsqrt(diag)


def tucker_kernel(
    chips, scale_x, scale_y,
    field_ref, fx_ref, fyt_ref, fzt_ref, ftt_ref,
    fx_out, fy_out, core_out,
    slots, w_ref, pp_ref, a_ref,
    part, other, y_all, qx_ref, s3, wy_send, wy_recv, wy_all, my_send, my_recv, fold, fold2, shares, pair_in, mine, landed,
    field_sem, pair_sem, gather_send, gather_recv, give_send, give_recv, wy_sem, core_send, core_recv,
):
    grp = lax.axis_index("grp")
    g = lax.axis_index("gx")
    h = lax.axis_index("gy")
    z = g // 4
    p = g % 4
    depth, pair = slots.shape[0], slots.shape[2]
    nt, nx = field_ref.shape[:2]
    nb, ra, nd = fyt_ref.shape[0], fx_ref.shape[1], ftt_ref.shape[0]
    nc = fzt_ref.shape[0]
    half = nb // 2 * LANES
    partner = (grp, g, 1 - h)

    def peer(chip):
        return (grp, chip, h)

    def fetch(i):
        slot = lax.rem(i, depth)
        return pltpu.make_async_copy(
            field_ref.at[:, pl.ds(i * pair, pair)], slots.at[slot], field_sem.at[slot]
        )

    steps = nx // pair
    for i in range(depth - 1):
        fetch(i).start()

    barrier = pltpu.get_barrier_semaphore()
    pl.semaphore_signal(barrier, inc=1, device_id=partner, device_id_type=MESH)
    for k in range(1, chips):
        pl.semaphore_signal(barrier, inc=1, device_id=peer((g + k) % chips), device_id_type=MESH)

    ftt = ftt_ref[...].astype(F32)
    fz = jnp.concatenate([fzt_ref[...].astype(F32)] * nd, axis=0).T
    ft = jnp.concatenate([jnp.broadcast_to(ftt[d : d + 1, :], (nc, nt)) for d in range(nd)], axis=0).T
    for t in range(nt):
        hi, lo = split2(fz * ft[t : t + 1, :])
        w_ref[t, :, :LANES] = hi
        w_ref[t, :, LANES:] = lo

    @pl.loop(0, steps)
    def _(i):
        @pl.when(i + depth - 1 < steps)
        def _():
            fetch(i + depth - 1).start()

        fetch(i).wait()
        slot = lax.rem(i, depth)
        for u in range(pair):
            acc = mm(slots[slot, 0, u], w_ref[0], NN)
            for t in range(1, nt):
                acc = acc + mm(slots[slot, t, u], w_ref[t], NN)
            hi, lo = split2(acc[:, :LANES] + acc[:, LANES:])
            pp = jnp.concatenate([hi, lo], axis=1)
            pp_ref[i * pair + u] = pp
            rows = mm(fyt_ref[...], pp, NN)
            a_ref[i * pair + u] = rows[:, :LANES] + rows[:, LANES:]

    for b in range(nb):
        part[:, b * LANES : (b + 1) * LANES] = a_ref[:, b, :]
    pl.semaphore_wait(barrier, chips)

    swap = pltpu.make_async_remote_copy(
        part, other, pair_sem.at[0], pair_sem.at[1], device_id=partner, device_id_type=MESH
    )
    swap.start()
    own = pl.ds(pl.multiple_of(g * nx, nx), nx)
    for s in range(2):
        y_all[s, own, half:] = jnp.zeros((nx, LANES), BF16)
        y_all[s, own, half : half + ra] = fx_ref[...]
    swap.wait()
    for s in range(2):
        at = slice(s * half, (s + 1) * half)
        y_all[s, own, :half] = (part[:, at] + other[:, at]).astype(BF16)

    along_x = p + 1 - 2 * (p % 2)
    along_y = (p + 2) % 4
    across = 3 - p
    planes = (p, along_x, along_y, across)
    columns = (slice(0, half + LANES), slice(0, half // 2), slice(half // 2, half + LANES))

    def chip_of(q, k):
        return ((z + 4 - k) % 4) * 4 + planes[q]

    def block(chip, side, cut):
        return y_all.at[side, pl.ds(pl.multiple_of(chip * nx, nx), nx), columns[cut]]

    def move(sems, q, k, cut, chip, side, target):
        i = q * 4 + k + (4 if cut == 2 else 0)
        ref = block(chip, side, cut)
        return pltpu.make_async_remote_copy(
            ref, ref, sems[0].at[i], sems[1].at[i], device_id=target, device_id_type=MESH
        )

    over_links, over_cores = (gather_send, gather_recv), (give_send, give_recv)
    started = []
    gives = []

    def send(q, k, cut, chip, target):
        c = move(over_links, q, k, cut, chip, h, peer(target))
        c.start()
        started.append(c)

    def arrived(q, k, cut):
        chip = chip_of(q, k)
        move(over_links, q, k, cut, chip, h, partner).wait_recv()
        c = move(over_cores, q, k, cut, chip, h, partner)
        c.start()
        gives.append((c, q, k, cut))

    def forward_whole(k):
        send(1, k, 0, chip_of(0, k), z * 4 + along_x)
        send(2, k, 0, chip_of(0, k), z * 4 + along_y)

    def forward_halves(k):
        arrived(1, k, 0)
        send(3, k, 2, chip_of(1, k), z * 4 + along_y)
        arrived(2, k, 0)
        send(3, k, 1, chip_of(2, k), z * 4 + along_x)

    for k in (1, 3, 2):
        send(0, k, 0, g, ((z + k) % 4) * 4 + p)
    forward_whole(0)
    arrived(0, 1, 0)
    forward_whole(1)
    forward_halves(0)
    arrived(0, 3, 0)
    forward_whole(3)
    forward_halves(1)
    arrived(0, 2, 0)
    forward_whole(2)
    forward_halves(3)
    forward_halves(2)
    for k in (0, 1, 3, 2):
        arrived(3, k, 1)
        arrived(3, k, 2)
    for c, q, k, cut in gives:
        move(over_cores, q, k, cut, chip_of(q, k), 1 - h, partner).wait_recv()
    for c in started:
        c.wait_send()
    for c, q, k, cut in gives:
        c.wait_send()

    left = y_all[0, :, :half]
    right = y_all[1, :, :half]
    gram = mm(left, left, NT) + mm(right, right, NT)
    old = y_all[0, :, half:][:, :ra].astype(F32)
    power_x = mm(gram, old, NN, HIGH)
    inv_x = inverse_lower(mm(power_x, power_x, TN, HIGH))
    qx = mm(power_x, inv_x, NT, HIGH)
    qx_ref[...] = qx
    q_own = qx_ref[own, :]
    fx_out[...] = scale_x * q_own
    onto = jnp.concatenate(split3(mm(q_own, qx, NT, HIGH)), axis=0)
    for s in range(2):
        spread = mm(onto, y_all[s, :, :half], NN)
        spread = spread[:nx] + spread[nx : 2 * nx] + spread[2 * nx :]
        for b in range(nb // 2):
            s3[s * (nb // 2) + b] = spread[:, b * LANES : (b + 1) * LANES]

    acc = jnp.zeros((2 * nb, pp_ref.shape[1]), F32)
    for x in range(nx):
        hi, lo = split2(s3[:, x, :])
        both = jnp.concatenate([jnp.concatenate([hi, hi], 1), jnp.concatenate([lo, lo], 1)], 0)
        acc = acc + mm(both, pp_ref[x], NT)
    power_y = acc[:nb] + acc[nb:]
    ny = power_y.shape[1]
    wide = ny // 4
    for c in range(chips):
        wy_send[c, :, :wide] = power_y[c // 4 * 8 : c // 4 * 8 + 8, c % 4 * wide : (c % 4 + 1) * wide]
        wy_send[c, :, wide:] = jnp.zeros((8, LANES - wide), F32)
    sends = []
    for k in range(1, chips):
        target = (g + k) % chips
        c = pltpu.make_async_remote_copy(
            wy_send.at[target], wy_recv.at[k], wy_sem.at[0, k], wy_sem.at[1, k],
            device_id=peer(target), device_id_type=MESH,
        )
        c.start()
        sends.append(c)
    piece = wy_send[g]
    for k, c in enumerate(sends):
        c.wait_recv()
        piece = piece + wy_recv[k + 1]
    wy_all[g] = piece

    def spread_piece(chip, k, target):
        return pltpu.make_async_remote_copy(
            wy_all.at[chip], wy_all.at[chip], wy_sem.at[2, k], wy_sem.at[3, k],
            device_id=target, device_id_type=MESH,
        )

    for k in range(1, chips):
        c = spread_piece(g, k, peer((g + k) % chips))
        c.start()
        sends.append(c)
    for k in range(1, chips):
        spread_piece((g + chips - k) % chips, k, partner).wait_recv()
    for c in sends:
        c.wait_send()
    power_y = jnp.concatenate(
        [
            jnp.concatenate([wy_all[r * 4 + u][:, :wide] for u in range(4)], axis=1)
            for r in range(nb // 8)
        ],
        axis=0,
    )

    my_send[...] = jnp.zeros(my_send.shape, F32)
    my_send[:, :nb] = mm(power_y, power_y, NT, HIGH)
    my_copy = pltpu.make_async_remote_copy(
        my_send, my_recv, pair_sem.at[2], pair_sem.at[3], device_id=partner, device_id_type=MESH
    )
    my_copy.start()

    wy2 = jnp.concatenate(split2(power_y), axis=0)
    for x in range(nx):
        f = mm(wy2, pp_ref[x], NN)
        f = f[:nb] + f[nb:]
        fold[x] = f[:, :LANES] + f[:, LANES:]
    for b in range(nb):
        fold2[:, b * LANES : (b + 1) * LANES] = fold[:, b, :]
    term = mm(q_own, fold2[...], TN, HIGH)
    for r in range(8):
        rows = jnp.concatenate(
            [term[:, (u * 8 + r) * LANES : (u * 8 + r + 1) * LANES] for u in range(nb // 8)], axis=0
        )
        shares[:, r, :] = rows.T
    mine_rows = shares.shape[0] // (2 * chips)
    pair_copies = []
    for c in range(chips):
        src = shares.at[pl.ds((c * 2 + 1 - h) * mine_rows, mine_rows)]
        cp = pltpu.make_async_remote_copy(
            src, pair_in.at[c], core_send.at[0, c], core_recv.at[0, c],
            device_id=partner, device_id_type=MESH,
        )
        cp.start()
        pair_copies.append(cp)
    for cp in pair_copies:
        cp.wait()
    for c in range(chips):
        mine[c] = shares[pl.ds((c * 2 + h) * mine_rows, mine_rows)] + pair_in[c]
    sends = []
    for k in range(1, chips):
        target = (g + k) % chips
        cp = pltpu.make_async_remote_copy(
            mine.at[target], landed.at[k], core_send.at[1, k], core_recv.at[1, k],
            device_id=peer(target), device_id_type=MESH,
        )
        cp.start()
        sends.append(cp)

    my_copy.wait()
    inv_y = inverse_lower(my_send[:, :nb] + my_recv[:, :nb])
    fy_out[...] = scale_y * mm(inv_y, power_y, NN, HIGH)

    for cp in sends:
        cp.wait()
    total = mine[g]
    for k in range(1, chips):
        total = total + landed[k]
    columns = [
        jnp.concatenate([total[i][:, u * ra : (u + 1) * ra] for u in range(nb // 8)], axis=0)
        for i in range(mine_rows)
    ]
    raw = jnp.concatenate(columns, axis=1)
    core_out[...] = mm(inv_y, raw, NN, HIGH)


def fast_body(chips, field, factor_x_old, factor_y_old, factor_z, factor_t):
    nt, nx, ny, nz = field.shape
    ra = factor_x_old.shape[1]
    nb = factor_y_old.shape[1]
    xs = nx * chips
    wide = nb * LANES
    rows = LANES // (2 * chips)
    vmem = pl.BlockSpec(memory_space=pltpu.VMEM)
    dma = pltpu.SemaphoreType.DMA
    factor_x, factor_y, core = pl.pallas_call(
        functools.partial(tucker_kernel, chips, math.sqrt(xs), math.sqrt(2 * ny)),
        in_specs=[pl.BlockSpec(memory_space=pl.ANY)] + [vmem] * 4,
        out_specs=[vmem] * 3,
        out_shape=[
            jax.ShapeDtypeStruct((nx, ra), F32),
            jax.ShapeDtypeStruct((nb, ny), F32),
            jax.ShapeDtypeStruct((nb, rows * ra), F32),
        ],
        scratch_shapes=[
            pltpu.VMEM((3, nt, 2, ny, nz), BF16),
            pltpu.VMEM((nt, nz, 2 * LANES), BF16),
            pltpu.VMEM((nx, ny, 2 * LANES), BF16),
            pltpu.VMEM((nx, nb, LANES), F32),
            pltpu.VMEM((nx, wide), F32),
            pltpu.VMEM((nx, wide), F32),
            pltpu.VMEM((2, xs, wide // 2 + LANES), BF16),
            pltpu.VMEM((xs, ra), F32),
            pltpu.VMEM((nb, nx, LANES), F32),
            pltpu.VMEM((chips, 8, LANES), F32),
            pltpu.VMEM((chips, 8, LANES), F32),
            pltpu.VMEM((chips, 8, LANES), F32),
            pltpu.VMEM((nb, LANES), F32),
            pltpu.VMEM((nb, LANES), F32),
            pltpu.VMEM((nx, nb, LANES), F32),
            pltpu.VMEM((nx, wide), F32),
            pltpu.VMEM((LANES, 8, LANES), F32),
            pltpu.VMEM((chips, rows, 8, LANES), F32),
            pltpu.VMEM((chips, rows, 8, LANES), F32),
            pltpu.VMEM((chips, rows, 8, LANES), F32),
            dma((3,)), dma((4,)), dma((24,)), dma((24,)), dma((24,)), dma((24,)), dma((4, chips)), dma((2, chips)), dma((2, chips)),
        ],
        compiler_params=pltpu.CompilerParams(
            collective_id=0, has_side_effects=True, vmem_limit_bytes=52 << 20
        ),
    )(field, factor_x_old, factor_y_old.T, factor_z.T, factor_t.T)
    return factor_x, factor_y.T, core.T


def orthonormal(power, gram):
    lower = jnp.linalg.cholesky(gram)
    return jax.scipy.linalg.solve_triangular(lower, power.T, lower=True).T


def body(field, factor_x_old, factor_y_old, factor_z, factor_t):
    highest = lax.Precision.HIGHEST
    rows_x = field.shape[1]
    rank_x = factor_x_old.shape[1]
    rank_y = factor_y_old.shape[1]
    rank_z = factor_z.shape[1]
    rank_t = factor_t.shape[1]
    partial_q = jnp.einsum("txyz,zc->txcy", field, factor_z, preferred_element_type=jnp.float32)
    projected = jnp.einsum(
        "td,txcy->dxcy", factor_t.astype(jnp.float32), partial_q, precision=highest
    )
    local_rows = jnp.einsum(
        "dxcy,yb->xdcb", projected, factor_y_old.astype(jnp.float32), precision=highest
    )
    local_rows = local_rows.reshape(rows_x, rank_t * rank_z * rank_y)
    summed = lax.psum(local_rows, "gy")
    mode_rows = summed.astype(jnp.bfloat16)
    mode_float = mode_rows.astype(jnp.float32)
    gram = lax.dot_general(
        mode_rows,
        lax.all_gather(mode_rows, "gx", axis=0, tiled=True),
        (((1,), (1,)), ((), ())),
        preferred_element_type=jnp.float32,
    )
    power_x = jnp.dot(
        gram,
        lax.all_gather(factor_x_old, "gx", axis=0, tiled=True).astype(jnp.float32),
        precision=highest,
    )
    gram_x = lax.psum(jnp.dot(power_x.T, power_x, precision=highest), "gx")
    basis_x = orthonormal(power_x, gram_x)
    core_x = lax.psum(jnp.dot(basis_x.T, mode_float, precision=highest), "gx")
    spread = jnp.dot(basis_x, core_x, precision=highest).reshape(rows_x, rank_t, rank_z, rank_y)
    part_y = jnp.einsum("dxcy,xdcb->yb", projected, spread, precision=highest)
    power_y = lax.psum(part_y, "gx")
    gram_y = lax.psum(jnp.dot(power_y.T, power_y, precision=highest), "gy")
    basis_y = orthonormal(power_y, gram_y)
    folded = jnp.einsum("dxcy,yb->dxcb", projected, basis_y, precision=highest)
    core_term = jnp.einsum("dxcb,xa->dcab", folded, basis_x, precision=highest).reshape(
        rank_t * rank_z * rank_x, rank_y
    )
    core = lax.psum_scatter(core_term, ("gx", "gy"), scatter_dimension=0, tiled=True)
    total_x = rows_x * lax.axis_size("gx")
    total_y = power_y.shape[0] * lax.axis_size("gy")
    return (math.sqrt(total_x) * basis_x, math.sqrt(total_y) * basis_y, core)


def solution(mesh):
    placed = (
        P(None, ("grp", "gx"), "gy", None),
        P(("grp", "gx"), None),
        P(("grp", "gy"), None),
        P(),
        P(),
    )
    chips = mesh.shape["gx"]

    def run(field, factor_x_old, factor_y_old, factor_z, factor_t):
        packed = factor_z.shape[1] * factor_t.shape[1]
        fits = (
            chips == 16
            and mesh.shape["gy"] == 2
            and packed == LANES
            and field.shape[1] == 16
            and factor_x_old.shape[1] == 32
            and factor_y_old.shape[1] == 32
            and field.shape[2] == 256
            and field.shape[3] % 256 == 0
        )
        if fits:
            return fast_body(chips, field, factor_x_old, factor_y_old, factor_z, factor_t)
        return body(field, factor_x_old, factor_y_old, factor_z, factor_t)

    return jax.shard_map(
        run,
        mesh=mesh,
        in_specs=placed,
        out_specs=(P(("grp", "gx"), None), P(("grp", "gy"), None), P(("grp", "gx", "gy"), None)),
        check_vma=False,
    )
```

```python
import functools
import math

import jax
import jax.numpy as jnp
from jax import lax
from jax.experimental import pallas as pl
from jax.experimental.pallas import tpu as pltpu
from jax.sharding import PartitionSpec as P

MESH = pl.DeviceIdType.MESH
HIGH = lax.Precision.HIGHEST
F32 = jnp.float32
BF16 = jnp.bfloat16
LANES = 128
NN = (((1,), (0,)), ((), ()))
NT = (((1,), (1,)), ((), ()))
TN = (((0,), (0,)), ((), ()))


def mm(a, b, dims, precision=None):
    return lax.dot_general(a, b, dims, precision=precision, preferred_element_type=F32)


def split2(v):
    hi = v.astype(BF16)
    return hi, (v - hi.astype(F32)).astype(BF16)


def split3(v):
    hi = v.astype(BF16)
    rest = v - hi.astype(F32)
    mid = rest.astype(BF16)
    return hi, mid, (rest - mid.astype(F32)).astype(BF16)


def inverse_lower(gram):
    n = gram.shape[0]
    row = lax.broadcasted_iota(jnp.int32, (n, n), 0)
    col = lax.broadcasted_iota(jnp.int32, (n, n), 1)
    eye = jnp.where(row == col, 1.0, 0.0).astype(F32)
    both = jnp.concatenate([gram, eye], axis=1)
    at = lax.broadcasted_iota(jnp.int32, (n, 1), 0)
    for j in range(n - 1):
        pivot_row = both[j : j + 1, :]
        scale = jnp.where(at > j, both[:, j : j + 1] / pivot_row[:, j : j + 1], 0.0)
        both = both - scale * pivot_row
    diag = jnp.sum(both[:, :n] * eye, axis=1, keepdims=True)
    return both[:, n:] * lax.rsqrt(diag)


def tucker_kernel(
    chips, scale_x, scale_y,
    field_ref, fx_in, fyt_in, fzt_in, ftt_in,
    fx_out, fy_out, core_out,
    fx_ref, fyt_ref, fzt_ref, ftt_ref, slots, w_ref, pp_ref, a_ref,
    part, other, y_all, qx_ref, s3, wy_all, my_send, my_recv, fold, fold2, shares, pair_in, mine, landed,
    field_sem, pair_sem, gather_send, gather_recv, give_send, give_recv, wy_sem, core_send, core_recv, small_sem,
):
    grp = lax.axis_index("grp")
    g = lax.axis_index("gx")
    h = lax.axis_index("gy")
    z = g // 4
    p = g % 4
    depth, pair = slots.shape[0], slots.shape[2]
    nt, nx = field_ref.shape[:2]
    nb, ra, nd = fyt_ref.shape[0], fx_ref.shape[1], ftt_ref.shape[0]
    nc = fzt_ref.shape[0]
    half = nb // 2 * LANES
    partner = (grp, g, 1 - h)

    def peer(chip):
        return (grp, chip, h)

    def fetch(i):
        slot = lax.rem(i, depth)
        return pltpu.make_async_copy(
            field_ref.at[:, pl.ds(i * pair, pair)], slots.at[slot], field_sem.at[slot]
        )

    small = [
        pltpu.make_async_copy(src, dst, small_sem.at[i])
        for i, (src, dst) in enumerate(
            ((fzt_in, fzt_ref), (ftt_in, ftt_ref), (fyt_in, fyt_ref), (fx_in, fx_ref))
        )
    ]
    for c in small:
        c.start()
    steps = nx // pair
    for i in range(depth - 1):
        fetch(i).start()

    barrier = pltpu.get_barrier_semaphore()
    pl.semaphore_signal(barrier, inc=1, device_id=partner, device_id_type=MESH)
    for k in range(1, chips):
        pl.semaphore_signal(barrier, inc=1, device_id=peer((g + k) % chips), device_id_type=MESH)

    for c in small:
        c.wait()

    ftt = ftt_ref[...].astype(F32)
    fz = jnp.concatenate([fzt_ref[...].astype(F32)] * nd, axis=0).T
    ft = jnp.concatenate([jnp.broadcast_to(ftt[d : d + 1, :], (nc, nt)) for d in range(nd)], axis=0).T
    for t in range(nt):
        hi, lo = split2(fz * ft[t : t + 1, :])
        w_ref[t, :, :LANES] = hi
        w_ref[t, :, LANES:] = lo

    @pl.loop(0, steps)
    def _(i):
        @pl.when(i + depth - 1 < steps)
        def _():
            fetch(i + depth - 1).start()

        fetch(i).wait()
        slot = lax.rem(i, depth)
        for u in range(pair):
            acc = mm(slots[slot, 0, u], w_ref[0], NN)
            for t in range(1, nt):
                acc = acc + mm(slots[slot, t, u], w_ref[t], NN)
            hi, lo = split2(acc[:, :LANES] + acc[:, LANES:])
            pp = jnp.concatenate([hi, lo], axis=1)
            pp_ref[i * pair + u] = pp
            rows = mm(fyt_ref[...], pp, NN)
            a_ref[i * pair + u] = rows[:, :LANES] + rows[:, LANES:]

    for b in range(nb):
        part[:, b * LANES : (b + 1) * LANES] = a_ref[:, b, :]
    pl.semaphore_wait(barrier, chips)

    swap = pltpu.make_async_remote_copy(
        part, other, pair_sem.at[0], pair_sem.at[1], device_id=partner, device_id_type=MESH
    )
    swap.start()
    own = pl.ds(pl.multiple_of(g * nx, nx), nx)
    for s in range(2):
        y_all[s, own, half:] = jnp.zeros((nx, LANES), BF16)
        y_all[s, own, half : half + ra] = fx_ref[...]
    swap.wait()
    for s in range(2):
        at = slice(s * half, (s + 1) * half)
        y_all[s, own, :half] = (part[:, at] + other[:, at]).astype(BF16)

    def block(chip, side):
        return y_all.at[side, pl.ds(pl.multiple_of(chip * nx, nx), nx), :]

    def chip_of(q, k):
        return ((z + 4 - k) % 4) * 4 + (p + q) % 4

    def gather(q, k, target, source):
        i = q * 4 + k
        return pltpu.make_async_remote_copy(
            block(source, h), block(source, h), gather_send.at[i], gather_recv.at[i],
            device_id=peer(target), device_id_type=MESH,
        )

    def give(q, k):
        i = q * 4 + k
        source = chip_of(q, k)
        return pltpu.make_async_remote_copy(
            block(source, h), block(source, h), give_send.at[i], give_recv.at[i],
            device_id=partner, device_id_type=MESH,
        )

    started = []
    for k in (1, 3, 2):
        c = gather(0, k, ((z + k) % 4) * 4 + p, g)
        c.start()
        started.append(c)
    for q in (1, 3, 2):
        c = gather(q, 0, z * 4 + (p + 4 - q) % 4, g)
        c.start()
        started.append(c)
    gives = []

    def arrived(q, k):
        i = q * 4 + k
        source = chip_of(q, k)
        pltpu.make_async_remote_copy(
            block(source, h), block(source, h), gather_send.at[i], gather_recv.at[i],
            device_id=partner, device_id_type=MESH,
        ).wait_recv()
        c = give(q, k)
        c.start()
        gives.append((c, q, k))

    for k in (1, 3, 2):
        arrived(0, k)
        for q in (1, 3, 2):
            c = gather(q, k, z * 4 + (p + 4 - q) % 4, chip_of(0, k))
            c.start()
            started.append(c)
    for k in (0, 1, 3, 2):
        for q in (1, 3, 2):
            arrived(q, k)
    for c, q, k in gives:
        i = q * 4 + k
        theirs = block(chip_of(q, k), 1 - h)
        pltpu.make_async_remote_copy(
            theirs, theirs, give_send.at[i], give_recv.at[i], device_id=partner, device_id_type=MESH
        ).wait_recv()
    for c in started:
        c.wait_send()
    for c, q, k in gives:
        c.wait_send()

    left = y_all[0, :, :half]
    right = y_all[1, :, :half]
    gram = mm(left, left, NT) + mm(right, right, NT)
    old = y_all[0, :, half:][:, :ra].astype(F32)
    power_x = mm(gram, old, NN, HIGH)
    inv_x = inverse_lower(mm(power_x, power_x, TN, HIGH))
    qx = mm(power_x, inv_x, NT, HIGH)
    qx_ref[...] = qx
    q_own = qx_ref[own, :]
    fx_out[...] = scale_x * q_own
    onto = jnp.concatenate(split3(mm(q_own, qx, NT, HIGH)), axis=0)
    for s in range(2):
        spread = mm(onto, y_all[s, :, :half], NN)
        spread = spread[:nx] + spread[nx : 2 * nx] + spread[2 * nx :]
        for b in range(nb // 2):
            s3[s * (nb // 2) + b] = spread[:, b * LANES : (b + 1) * LANES]

    acc = jnp.zeros((2 * nb, pp_ref.shape[1]), F32)
    for x in range(nx):
        hi, lo = split2(s3[:, x, :])
        both = jnp.concatenate([jnp.concatenate([hi, hi], 1), jnp.concatenate([lo, lo], 1)], 0)
        acc = acc + mm(both, pp_ref[x], NT)
    power_y = acc[:nb] + acc[nb:]
    sends = []
    for phase, at in ((0, p), (1, z)):
        wy_all[phase, at] = power_y

        def exchange(k, target, source):
            ref = wy_all.at[phase, source]
            return pltpu.make_async_remote_copy(
                ref, ref, wy_sem.at[2 * phase, k], wy_sem.at[2 * phase + 1, k],
                device_id=target, device_id_type=MESH,
            )

        for k in (1, 3, 2):
            to = (at + k) % 4
            c = exchange(k, peer(z * 4 + to if phase == 0 else to * 4 + p), at)
            c.start()
            sends.append(c)
        for k in (1, 3, 2):
            exchange(k, partner, (at + 4 - k) % 4).wait_recv()
        power_y = (wy_all[phase, 0] + wy_all[phase, 1]) + (wy_all[phase, 2] + wy_all[phase, 3])
    for c in sends:
        c.wait_send()

    my_send[...] = jnp.zeros(my_send.shape, F32)
    my_send[:, :nb] = mm(power_y, power_y, NT, HIGH)
    my_copy = pltpu.make_async_remote_copy(
        my_send, my_recv, pair_sem.at[2], pair_sem.at[3], device_id=partner, device_id_type=MESH
    )
    my_copy.start()

    wy2 = jnp.concatenate(split2(power_y), axis=0)
    for x in range(nx):
        f = mm(wy2, pp_ref[x], NN)
        f = f[:nb] + f[nb:]
        fold[x] = f[:, :LANES] + f[:, LANES:]
    for b in range(nb):
        fold2[:, b * LANES : (b + 1) * LANES] = fold[:, b, :]
    term = mm(q_own, fold2[...], TN, HIGH)
    for r in range(8):
        rows = jnp.concatenate(
            [term[:, (u * 8 + r) * LANES : (u * 8 + r + 1) * LANES] for u in range(nb // 8)], axis=0
        )
        shares[:, r, :] = rows.T
    mine_rows = shares.shape[0] // (2 * chips)
    pair_copies = []
    for c in range(chips):
        src = shares.at[pl.ds((c * 2 + 1 - h) * mine_rows, mine_rows)]
        cp = pltpu.make_async_remote_copy(
            src, pair_in.at[c], core_send.at[0, c], core_recv.at[0, c],
            device_id=partner, device_id_type=MESH,
        )
        cp.start()
        pair_copies.append(cp)
    for cp in pair_copies:
        cp.wait()
    for c in range(chips):
        mine[c] = shares[pl.ds((c * 2 + h) * mine_rows, mine_rows)] + pair_in[c]
    sends = []
    for k in range(1, chips):
        target = (g + k) % chips
        cp = pltpu.make_async_remote_copy(
            mine.at[target], landed.at[k], core_send.at[1, k], core_recv.at[1, k],
            device_id=peer(target), device_id_type=MESH,
        )
        cp.start()
        sends.append(cp)

    my_copy.wait()
    inv_y = inverse_lower(my_send[:, :nb] + my_recv[:, :nb])
    fy_out[...] = scale_y * mm(inv_y, power_y, NN, HIGH)

    for cp in sends:
        cp.wait()
    total = mine[g]
    for k in range(1, chips):
        total = total + landed[k]
    columns = [
        jnp.concatenate([total[i][:, u * ra : (u + 1) * ra] for u in range(nb // 8)], axis=0)
        for i in range(mine_rows)
    ]
    raw = jnp.concatenate(columns, axis=1)
    core_out[...] = mm(inv_y, raw, NN, HIGH)


def fast_body(chips, field, factor_x_old, factor_y_old, factor_z, factor_t):
    nt, nx, ny, nz = field.shape
    ra = factor_x_old.shape[1]
    nb = factor_y_old.shape[1]
    xs = nx * chips
    wide = nb * LANES
    rows = LANES // (2 * chips)
    vmem = pl.BlockSpec(memory_space=pltpu.VMEM)
    dma = pltpu.SemaphoreType.DMA
    factor_x, factor_y, core = pl.pallas_call(
        functools.partial(tucker_kernel, chips, math.sqrt(xs), math.sqrt(2 * ny)),
        in_specs=[pl.BlockSpec(memory_space=pltpu.HBM)] * 5,
        out_specs=[vmem] * 3,
        out_shape=[
            jax.ShapeDtypeStruct((nx, ra), F32),
            jax.ShapeDtypeStruct((nb, ny), F32),
            jax.ShapeDtypeStruct((nb, rows * ra), F32),
        ],
        scratch_shapes=[
            pltpu.VMEM((nx, ra), BF16),
            pltpu.VMEM((nb, ny), BF16),
            pltpu.VMEM(factor_z.shape[::-1], BF16),
            pltpu.VMEM(factor_t.shape[::-1], BF16),
            pltpu.VMEM((5, nt, 2, ny, nz), BF16),
            pltpu.VMEM((nt, nz, 2 * LANES), BF16),
            pltpu.VMEM((nx, ny, 2 * LANES), BF16),
            pltpu.VMEM((nx, nb, LANES), F32),
            pltpu.VMEM((nx, wide), F32),
            pltpu.VMEM((nx, wide), F32),
            pltpu.VMEM((2, xs, wide // 2 + LANES), BF16),
            pltpu.VMEM((xs, ra), F32),
            pltpu.VMEM((nb, nx, LANES), F32),
            pltpu.VMEM((2, 4, nb, ny), F32),
            pltpu.VMEM((nb, LANES), F32),
            pltpu.VMEM((nb, LANES), F32),
            pltpu.VMEM((nx, nb, LANES), F32),
            pltpu.VMEM((nx, wide), F32),
            pltpu.VMEM((LANES, 8, LANES), F32),
            pltpu.VMEM((chips, rows, 8, LANES), F32),
            pltpu.VMEM((chips, rows, 8, LANES), F32),
            pltpu.VMEM((chips, rows, 8, LANES), F32),
            dma((5,)), dma((4,)), dma((16,)), dma((16,)), dma((16,)), dma((16,)), dma((4, 4)), dma((2, chips)), dma((2, chips)), dma((4,)),
        ],
        compiler_params=pltpu.CompilerParams(
            collective_id=0, has_side_effects=True, vmem_limit_bytes=52 << 20
        ),
    )(field, factor_x_old, factor_y_old.T, factor_z.T, factor_t.T)
    return factor_x, factor_y.T, core.T


def orthonormal(power, gram):
    lower = jnp.linalg.cholesky(gram)
    return jax.scipy.linalg.solve_triangular(lower, power.T, lower=True).T


def body(field, factor_x_old, factor_y_old, factor_z, factor_t):
    highest = lax.Precision.HIGHEST
    rows_x = field.shape[1]
    rank_x = factor_x_old.shape[1]
    rank_y = factor_y_old.shape[1]
    rank_z = factor_z.shape[1]
    rank_t = factor_t.shape[1]
    partial_q = jnp.einsum("txyz,zc->txcy", field, factor_z, preferred_element_type=jnp.float32)
    projected = jnp.einsum(
        "td,txcy->dxcy", factor_t.astype(jnp.float32), partial_q, precision=highest
    )
    local_rows = jnp.einsum(
        "dxcy,yb->xdcb", projected, factor_y_old.astype(jnp.float32), precision=highest
    )
    local_rows = local_rows.reshape(rows_x, rank_t * rank_z * rank_y)
    summed = lax.psum(local_rows, "gy")
    mode_rows = summed.astype(jnp.bfloat16)
    mode_float = mode_rows.astype(jnp.float32)
    gram = lax.dot_general(
        mode_rows,
        lax.all_gather(mode_rows, "gx", axis=0, tiled=True),
        (((1,), (1,)), ((), ())),
        preferred_element_type=jnp.float32,
    )
    power_x = jnp.dot(
        gram,
        lax.all_gather(factor_x_old, "gx", axis=0, tiled=True).astype(jnp.float32),
        precision=highest,
    )
    gram_x = lax.psum(jnp.dot(power_x.T, power_x, precision=highest), "gx")
    basis_x = orthonormal(power_x, gram_x)
    core_x = lax.psum(jnp.dot(basis_x.T, mode_float, precision=highest), "gx")
    spread = jnp.dot(basis_x, core_x, precision=highest).reshape(rows_x, rank_t, rank_z, rank_y)
    part_y = jnp.einsum("dxcy,xdcb->yb", projected, spread, precision=highest)
    power_y = lax.psum(part_y, "gx")
    gram_y = lax.psum(jnp.dot(power_y.T, power_y, precision=highest), "gy")
    basis_y = orthonormal(power_y, gram_y)
    folded = jnp.einsum("dxcy,yb->dxcb", projected, basis_y, precision=highest)
    core_term = jnp.einsum("dxcb,xa->dcab", folded, basis_x, precision=highest).reshape(
        rank_t * rank_z * rank_x, rank_y
    )
    core = lax.psum_scatter(core_term, ("gx", "gy"), scatter_dimension=0, tiled=True)
    total_x = rows_x * lax.axis_size("gx")
    total_y = power_y.shape[0] * lax.axis_size("gy")
    return (math.sqrt(total_x) * basis_x, math.sqrt(total_y) * basis_y, core)


def solution(mesh):
    placed = (
        P(None, ("grp", "gx"), "gy", None),
        P(("grp", "gx"), None),
        P(("grp", "gy"), None),
        P(),
        P(),
    )
    chips = mesh.shape["gx"]

    def run(field, factor_x_old, factor_y_old, factor_z, factor_t):
        packed = factor_z.shape[1] * factor_t.shape[1]
        fits = (
            chips == 16
            and mesh.shape["gy"] == 2
            and packed == LANES
            and field.shape[1] == 16
            and factor_x_old.shape[1] == 32
            and factor_y_old.shape[1] == 32
            and field.shape[2] == 256
            and field.shape[3] % 256 == 0
        )
        if fits:
            return fast_body(chips, field, factor_x_old, factor_y_old, factor_z, factor_t)
        return body(field, factor_x_old, factor_y_old, factor_z, factor_t)

    return jax.shard_map(
        run,
        mesh=mesh,
        in_specs=placed,
        out_specs=(P(("grp", "gx"), None), P(("grp", "gy"), None), P(("grp", "gx", "gy"), None)),
        check_vma=False,
    )
```

```python
import functools
import math

import jax
import jax.numpy as jnp
from jax import lax
from jax.experimental import pallas as pl
from jax.experimental.pallas import tpu as pltpu
from jax.sharding import PartitionSpec as P

MESH = pl.DeviceIdType.MESH
HIGH = lax.Precision.HIGHEST
F32 = jnp.float32
BF16 = jnp.bfloat16
LANES = 128
NN = (((1,), (0,)), ((), ()))
NT = (((1,), (1,)), ((), ()))
TN = (((0,), (0,)), ((), ()))


def mm(a, b, dims, precision=None):
    return lax.dot_general(a, b, dims, precision=precision, preferred_element_type=F32)


def split2(v):
    hi = v.astype(BF16)
    return hi, (v - hi.astype(F32)).astype(BF16)


def split3(v):
    hi = v.astype(BF16)
    rest = v - hi.astype(F32)
    mid = rest.astype(BF16)
    return hi, mid, (rest - mid.astype(F32)).astype(BF16)


def inverse_lower(gram):
    n = gram.shape[0]
    row = lax.broadcasted_iota(jnp.int32, (n, n), 0)
    col = lax.broadcasted_iota(jnp.int32, (n, n), 1)
    eye = jnp.where(row == col, 1.0, 0.0).astype(F32)
    both = jnp.concatenate([gram, eye], axis=1)
    at = lax.broadcasted_iota(jnp.int32, (n, 1), 0)
    for j in range(n - 1):
        pivot_row = both[j : j + 1, :]
        scale = jnp.where(at > j, both[:, j : j + 1] / pivot_row[:, j : j + 1], 0.0)
        both = both - scale * pivot_row
    diag = jnp.sum(both[:, :n] * eye, axis=1, keepdims=True)
    return both[:, n:] * lax.rsqrt(diag)


def tucker_kernel(
    chips, scale_x, scale_y,
    field_ref, fx_in, fyt_in, fzt_in, ftt_in,
    fx_out, fy_out, core_out,
    fx_ref, fyt_ref, fzt_ref, ftt_ref, slots, w_ref, pp_ref, a_ref,
    part, other, y_all, qx_ref, s3, wy_all, my_send, my_recv, fold, fold2, shares, pair_in, mine, landed,
    field_sem, pair_sem, gather_send, gather_recv, give_send, give_recv, wy_sem, core_send, core_recv, small_sem,
):
    grp = lax.axis_index("grp")
    g = lax.axis_index("gx")
    h = lax.axis_index("gy")
    z = g // 4
    p = g % 4
    depth, pair = slots.shape[0], slots.shape[2]
    nt, nx = field_ref.shape[:2]
    nb, ra, nd = fyt_ref.shape[0], fx_ref.shape[1], ftt_ref.shape[0]
    nc = fzt_ref.shape[0]
    half = nb // 2 * LANES
    partner = (grp, g, 1 - h)

    def peer(chip):
        return (grp, chip, h)

    def fetch(i):
        slot = lax.rem(i, depth)
        return pltpu.make_async_copy(
            field_ref.at[:, pl.ds(i * pair, pair)], slots.at[slot], field_sem.at[slot]
        )

    small = [
        pltpu.make_async_copy(src, dst, small_sem.at[i])
        for i, (src, dst) in enumerate(
            ((fzt_in, fzt_ref), (ftt_in, ftt_ref), (fyt_in, fyt_ref), (fx_in, fx_ref))
        )
    ]
    for c in small:
        c.start()
    steps = nx // pair
    for i in range(depth - 1):
        fetch(i).start()

    barrier = pltpu.get_barrier_semaphore()
    pl.semaphore_signal(barrier, inc=1, device_id=partner, device_id_type=MESH)
    for k in range(1, chips):
        pl.semaphore_signal(barrier, inc=1, device_id=peer((g + k) % chips), device_id_type=MESH)

    for c in small:
        c.wait()

    ftt = ftt_ref[...].astype(F32)
    fz = jnp.concatenate([fzt_ref[...].astype(F32)] * nd, axis=0).T
    ft = jnp.concatenate([jnp.broadcast_to(ftt[d : d + 1, :], (nc, nt)) for d in range(nd)], axis=0).T
    for t in range(nt):
        hi, lo = split2(fz * ft[t : t + 1, :])
        w_ref[t, :, :LANES] = hi
        w_ref[t, :, LANES:] = lo

    @pl.loop(0, steps)
    def _(i):
        @pl.when(i + depth - 1 < steps)
        def _():
            fetch(i + depth - 1).start()

        fetch(i).wait()
        slot = lax.rem(i, depth)
        for u in range(pair):
            acc = mm(slots[slot, 0, u], w_ref[0], NN)
            for t in range(1, nt):
                acc = acc + mm(slots[slot, t, u], w_ref[t], NN)
            hi, lo = split2(acc[:, :LANES] + acc[:, LANES:])
            pp = jnp.concatenate([hi, lo], axis=1)
            pp_ref[i * pair + u] = pp
            rows = mm(fyt_ref[...], pp, NN)
            a_ref[i * pair + u] = rows[:, :LANES] + rows[:, LANES:]

    for b in range(nb):
        part[:, b * LANES : (b + 1) * LANES] = a_ref[:, b, :]
    pl.semaphore_wait(barrier, chips)

    swap = pltpu.make_async_remote_copy(
        part, other, pair_sem.at[0], pair_sem.at[1], device_id=partner, device_id_type=MESH
    )
    swap.start()
    own = pl.ds(pl.multiple_of(g * nx, nx), nx)
    for s in range(2):
        y_all[s, own, half:] = jnp.zeros((nx, LANES), BF16)
        y_all[s, own, half : half + ra] = fx_ref[...]
    swap.wait()
    for s in range(2):
        at = slice(s * half, (s + 1) * half)
        y_all[s, own, :half] = (part[:, at] + other[:, at]).astype(BF16)

    def block(chip, side):
        return y_all.at[side, pl.ds(pl.multiple_of(chip * nx, nx), nx), :]

    def chip_of(q, k):
        return ((z + 4 - k) % 4) * 4 + (p + q) % 4

    def gather(q, k, target, source):
        i = q * 4 + k
        return pltpu.make_async_remote_copy(
            block(source, h), block(source, h), gather_send.at[i], gather_recv.at[i],
            device_id=peer(target), device_id_type=MESH,
        )

    def give(q, k):
        i = q * 4 + k
        source = chip_of(q, k)
        return pltpu.make_async_remote_copy(
            block(source, h), block(source, h), give_send.at[i], give_recv.at[i],
            device_id=partner, device_id_type=MESH,
        )

    started = []
    for k in (1, 3, 2):
        c = gather(0, k, ((z + k) % 4) * 4 + p, g)
        c.start()
        started.append(c)
    for q in (1, 3, 2):
        c = gather(q, 0, z * 4 + (p + 4 - q) % 4, g)
        c.start()
        started.append(c)
    gives = []

    def arrived(q, k):
        i = q * 4 + k
        source = chip_of(q, k)
        pltpu.make_async_remote_copy(
            block(source, h), block(source, h), gather_send.at[i], gather_recv.at[i],
            device_id=partner, device_id_type=MESH,
        ).wait_recv()
        c = give(q, k)
        c.start()
        gives.append((c, q, k))

    for k in (1, 3, 2):
        arrived(0, k)
        for q in (1, 3, 2):
            c = gather(q, k, z * 4 + (p + 4 - q) % 4, chip_of(0, k))
            c.start()
            started.append(c)
    for k in (0, 1, 3, 2):
        for q in (1, 3, 2):
            arrived(q, k)
    for c, q, k in gives:
        i = q * 4 + k
        theirs = block(chip_of(q, k), 1 - h)
        pltpu.make_async_remote_copy(
            theirs, theirs, give_send.at[i], give_recv.at[i], device_id=partner, device_id_type=MESH
        ).wait_recv()
    for c in started:
        c.wait_send()
    for c, q, k in gives:
        c.wait_send()

    left = y_all[0, :, :half]
    right = y_all[1, :, :half]
    gram = mm(left, left, NT) + mm(right, right, NT)
    old = y_all[0, :, half:][:, :ra].astype(F32)
    power_x = mm(gram, old, NN, HIGH)
    inv_x = inverse_lower(mm(power_x, power_x, TN, HIGH))
    qx = mm(power_x, inv_x, NT, HIGH)
    qx_ref[...] = qx
    q_own = qx_ref[own, :]
    fx_out[...] = scale_x * q_own
    onto = jnp.concatenate(split3(mm(q_own, qx, NT, HIGH)), axis=0)
    for s in range(2):
        spread = mm(onto, y_all[s, :, :half], NN)
        spread = spread[:nx] + spread[nx : 2 * nx] + spread[2 * nx :]
        for b in range(nb // 2):
            s3[s * (nb // 2) + b] = spread[:, b * LANES : (b + 1) * LANES]

    acc = jnp.zeros((2 * nb, pp_ref.shape[1]), F32)
    for x in range(nx):
        hi, lo = split2(s3[:, x, :])
        both = jnp.concatenate([jnp.concatenate([hi, hi], 1), jnp.concatenate([lo, lo], 1)], 0)
        acc = acc + mm(both, pp_ref[x], NT)
    power_y = acc[:nb] + acc[nb:]
    sends = []
    for phase, at in ((0, p), (1, z)):
        wy_all[phase, at] = power_y

        def exchange(k, target, source):
            ref = wy_all.at[phase, source]
            return pltpu.make_async_remote_copy(
                ref, ref, wy_sem.at[2 * phase, k], wy_sem.at[2 * phase + 1, k],
                device_id=target, device_id_type=MESH,
            )

        for k in (1, 3, 2):
            to = (at + k) % 4
            c = exchange(k, peer(z * 4 + to if phase == 0 else to * 4 + p), at)
            c.start()
            sends.append(c)
        for k in (1, 3, 2):
            exchange(k, partner, (at + 4 - k) % 4).wait_recv()
        power_y = (wy_all[phase, 0] + wy_all[phase, 1]) + (wy_all[phase, 2] + wy_all[phase, 3])
    for c in sends:
        c.wait_send()

    my_send[...] = jnp.zeros(my_send.shape, F32)
    my_send[:, :nb] = mm(power_y, power_y, NT, HIGH)
    my_copy = pltpu.make_async_remote_copy(
        my_send, my_recv, pair_sem.at[2], pair_sem.at[3], device_id=partner, device_id_type=MESH
    )
    my_copy.start()

    wy2 = jnp.concatenate(split2(power_y), axis=0)
    for x in range(nx):
        f = mm(wy2, pp_ref[x], NN)
        f = f[:nb] + f[nb:]
        fold[x] = f[:, :LANES] + f[:, LANES:]
    for b in range(nb):
        fold2[:, b * LANES : (b + 1) * LANES] = fold[:, b, :]
    term = mm(q_own, fold2[...], TN, HIGH)
    for r in range(8):
        rows = jnp.concatenate(
            [term[:, (u * 8 + r) * LANES : (u * 8 + r + 1) * LANES] for u in range(nb // 8)], axis=0
        )
        shares[:, r, :] = rows.T
    mine_rows = shares.shape[0] // (2 * chips)
    pair_copies = []
    for c in range(chips):
        src = shares.at[pl.ds((c * 2 + 1 - h) * mine_rows, mine_rows)]
        cp = pltpu.make_async_remote_copy(
            src, pair_in.at[c], core_send.at[0, c], core_recv.at[0, c],
            device_id=partner, device_id_type=MESH,
        )
        cp.start()
        pair_copies.append(cp)
    for cp in pair_copies:
        cp.wait()
    for c in range(chips):
        mine[c] = shares[pl.ds((c * 2 + h) * mine_rows, mine_rows)] + pair_in[c]
    sends = []
    for k in range(1, chips):
        target = (g + k) % chips
        cp = pltpu.make_async_remote_copy(
            mine.at[target], landed.at[k], core_send.at[1, k], core_recv.at[1, k],
            device_id=peer(target), device_id_type=MESH,
        )
        cp.start()
        sends.append(cp)

    my_copy.wait()
    inv_y = inverse_lower(my_send[:, :nb] + my_recv[:, :nb])
    fy_out[...] = scale_y * mm(inv_y, power_y, NN, HIGH)

    for cp in sends:
        cp.wait()
    total = mine[g]
    for k in range(1, chips):
        total = total + landed[k]
    columns = [
        jnp.concatenate([total[i][:, u * ra : (u + 1) * ra] for u in range(nb // 8)], axis=0)
        for i in range(mine_rows)
    ]
    raw = jnp.concatenate(columns, axis=1)
    core_out[...] = mm(inv_y, raw, NN, HIGH)


def finish_kernel(fx_ref, fy_ref, core_ref, fx_out, fy_out, core_out):
    fx_out[...] = fx_ref[...]
    fy_out[...] = fy_ref[...]
    core_out[...] = core_ref[...]


def fast_body(chips, field, factor_x_old, factor_y_old, factor_z, factor_t):
    nt, nx, ny, nz = field.shape
    ra = factor_x_old.shape[1]
    nb = factor_y_old.shape[1]
    xs = nx * chips
    wide = nb * LANES
    rows = LANES // (2 * chips)
    vmem = pl.BlockSpec(memory_space=pltpu.VMEM)
    dma = pltpu.SemaphoreType.DMA
    factor_x, factor_y, core = pl.pallas_call(
        functools.partial(tucker_kernel, chips, math.sqrt(xs), math.sqrt(2 * ny)),
        in_specs=[pl.BlockSpec(memory_space=pltpu.HBM)] * 5,
        out_specs=[vmem] * 3,
        out_shape=[
            jax.ShapeDtypeStruct((nx, ra), F32),
            jax.ShapeDtypeStruct((nb, ny), F32),
            jax.ShapeDtypeStruct((nb, rows * ra), F32),
        ],
        scratch_shapes=[
            pltpu.VMEM((nx, ra), BF16),
            pltpu.VMEM((nb, ny), BF16),
            pltpu.VMEM(factor_z.shape[::-1], BF16),
            pltpu.VMEM(factor_t.shape[::-1], BF16),
            pltpu.VMEM((5, nt, 2, ny, nz), BF16),
            pltpu.VMEM((nt, nz, 2 * LANES), BF16),
            pltpu.VMEM((nx, ny, 2 * LANES), BF16),
            pltpu.VMEM((nx, nb, LANES), F32),
            pltpu.VMEM((nx, wide), F32),
            pltpu.VMEM((nx, wide), F32),
            pltpu.VMEM((2, xs, wide // 2 + LANES), BF16),
            pltpu.VMEM((xs, ra), F32),
            pltpu.VMEM((nb, nx, LANES), F32),
            pltpu.VMEM((2, 4, nb, ny), F32),
            pltpu.VMEM((nb, LANES), F32),
            pltpu.VMEM((nb, LANES), F32),
            pltpu.VMEM((nx, nb, LANES), F32),
            pltpu.VMEM((nx, wide), F32),
            pltpu.VMEM((LANES, 8, LANES), F32),
            pltpu.VMEM((chips, rows, 8, LANES), F32),
            pltpu.VMEM((chips, rows, 8, LANES), F32),
            pltpu.VMEM((chips, rows, 8, LANES), F32),
            dma((5,)), dma((4,)), dma((16,)), dma((16,)), dma((16,)), dma((16,)), dma((4, 4)), dma((2, chips)), dma((2, chips)), dma((4,)),
        ],
        compiler_params=pltpu.CompilerParams(
            collective_id=0, has_side_effects=True, vmem_limit_bytes=52 << 20
        ),
    )(field, factor_x_old, factor_y_old.T, factor_z.T, factor_t.T)
    made = (factor_x, factor_y, core)
    factor_x, factor_y, core = pl.pallas_call(
        finish_kernel,
        in_specs=[vmem] * 3,
        out_specs=[vmem] * 3,
        out_shape=[jax.ShapeDtypeStruct(v.shape, F32) for v in made],
    )(*made)
    return factor_x, factor_y.T, core.T


def orthonormal(power, gram):
    lower = jnp.linalg.cholesky(gram)
    return jax.scipy.linalg.solve_triangular(lower, power.T, lower=True).T


def body(field, factor_x_old, factor_y_old, factor_z, factor_t):
    highest = lax.Precision.HIGHEST
    rows_x = field.shape[1]
    rank_x = factor_x_old.shape[1]
    rank_y = factor_y_old.shape[1]
    rank_z = factor_z.shape[1]
    rank_t = factor_t.shape[1]
    partial_q = jnp.einsum("txyz,zc->txcy", field, factor_z, preferred_element_type=jnp.float32)
    projected = jnp.einsum(
        "td,txcy->dxcy", factor_t.astype(jnp.float32), partial_q, precision=highest
    )
    local_rows = jnp.einsum(
        "dxcy,yb->xdcb", projected, factor_y_old.astype(jnp.float32), precision=highest
    )
    local_rows = local_rows.reshape(rows_x, rank_t * rank_z * rank_y)
    summed = lax.psum(local_rows, "gy")
    mode_rows = summed.astype(jnp.bfloat16)
    mode_float = mode_rows.astype(jnp.float32)
    gram = lax.dot_general(
        mode_rows,
        lax.all_gather(mode_rows, "gx", axis=0, tiled=True),
        (((1,), (1,)), ((), ())),
        preferred_element_type=jnp.float32,
    )
    power_x = jnp.dot(
        gram,
        lax.all_gather(factor_x_old, "gx", axis=0, tiled=True).astype(jnp.float32),
        precision=highest,
    )
    gram_x = lax.psum(jnp.dot(power_x.T, power_x, precision=highest), "gx")
    basis_x = orthonormal(power_x, gram_x)
    core_x = lax.psum(jnp.dot(basis_x.T, mode_float, precision=highest), "gx")
    spread = jnp.dot(basis_x, core_x, precision=highest).reshape(rows_x, rank_t, rank_z, rank_y)
    part_y = jnp.einsum("dxcy,xdcb->yb", projected, spread, precision=highest)
    power_y = lax.psum(part_y, "gx")
    gram_y = lax.psum(jnp.dot(power_y.T, power_y, precision=highest), "gy")
    basis_y = orthonormal(power_y, gram_y)
    folded = jnp.einsum("dxcy,yb->dxcb", projected, basis_y, precision=highest)
    core_term = jnp.einsum("dxcb,xa->dcab", folded, basis_x, precision=highest).reshape(
        rank_t * rank_z * rank_x, rank_y
    )
    core = lax.psum_scatter(core_term, ("gx", "gy"), scatter_dimension=0, tiled=True)
    total_x = rows_x * lax.axis_size("gx")
    total_y = power_y.shape[0] * lax.axis_size("gy")
    return (math.sqrt(total_x) * basis_x, math.sqrt(total_y) * basis_y, core)


def solution(mesh):
    placed = (
        P(None, ("grp", "gx"), "gy", None),
        P(("grp", "gx"), None),
        P(("grp", "gy"), None),
        P(),
        P(),
    )
    chips = mesh.shape["gx"]

    def run(field, factor_x_old, factor_y_old, factor_z, factor_t):
        packed = factor_z.shape[1] * factor_t.shape[1]
        fits = (
            chips == 16
            and mesh.shape["gy"] == 2
            and packed == LANES
            and field.shape[1] == 16
            and factor_x_old.shape[1] == 32
            and factor_y_old.shape[1] == 32
            and field.shape[2] == 256
            and field.shape[3] % 256 == 0
        )
        if fits:
            return fast_body(chips, field, factor_x_old, factor_y_old, factor_z, factor_t)
        return body(field, factor_x_old, factor_y_old, factor_z, factor_t)

    return jax.shard_map(
        run,
        mesh=mesh,
        in_specs=placed,
        out_specs=(P(("grp", "gx"), None), P(("grp", "gy"), None), P(("grp", "gx", "gy"), None)),
        check_vma=False,
    )
```
